32 devices in a mesh: group: 2 (over x), ep: 16 (over z, y, core).
Axes of the slice: x: 2, y: 2, z: 4, core: 2. Of those that a mesh axis runs over, the one named last changes fastest.
Arguments:
- tokens: bfloat16 [4096, 4096], P(('group', 'ep')), parts along dimension 0, may hold values from -6 to 6
- expert_ids: int32 [4096, 8], P(('group', 'ep')), parts along dimension 0, may hold values from 0 to 15, all different within a row; in each aligned block of 128 rows (0 to 127, 128 to 255, ...) at most 80 rows name the same one
- route_weights: bfloat16 [4096, 8], P(('group', 'ep')), parts along dimension 0, may hold values from 0.049804688 to 1
- smooth: float32 [4096], replicated, may hold values from 0.3 to 3
- gate_weight: bfloat16 [16, 4096, 768], P('ep'), may hold values from -0.09375 to 0.09375
- up_weight: bfloat16 [16, 4096, 768], P('ep'), may hold values from -0.09375 to 0.09375
- down_weight: bfloat16 [16, 768, 4096], P('ep'), may hold values from -0.21875 to 0.21875
Outputs:
- mixed: bfloat16 [4096, 4096], P(('group', 'ep')), parts along dimension 0
The draws below stay inside these ranges and needn't reach their ends.
There are 2 independent parts, one for each index of `group`. The reference program is written for one: setup_inputs(seed, part) draws one part's arguments, and reference() takes and returns one part's arrays. A program takes and returns all parts, laid end to end along the dimension named above; an argument that names none is the same for every part. Nothing has to cross between parts.
Inputs may be any that keep to these rules, and one draw needn't show every extreme that they name: `expert_ids`: A row's 8 ids are distinct. In each aligned block of 128 rows (the rows of one device) no expert is named by more than 80 rows, a bound that some block reaches.
All inputs are finite; a program needn't handle non-finite values.
Results may differ from the reference program's by a relative error of at most 0.007.
Values may be sent and summed in bfloat16 or wider, within the bound.
A program may use at most 128 MiB of HBM per device.

```python
import math
import jax
import jax.numpy as jnp
import numpy as np
from jax import lax

D = 4096
FF = 768
TOPK = 8
TOK_DEV = 128
TOKENS = 2048
EXPERTS = 16
CAP = 80
N_EP = 16


def level_of(own_key, shape, split, least, largest):
    gain = 1.0
    for axis_at, parts in split:
        heights = jax.random.uniform(jax.random.fold_in(jax.random.fold_in(own_key, 6), axis_at), (parts,), jnp.float32, least / len(split), largest / len(split))
        gain = gain * jnp.repeat(jnp.exp(heights), shape[axis_at] // parts).reshape((-1,) + (1,) * (len(shape) - 1 - axis_at))
    return gain


def assign_block(key, own, number, rows, amount, top, reach, skew):
    order = jax.random.permutation(key, amount)
    packed, common = load_shares(amount, rows * top, reach, skew, True), load_shares(amount, rows * top, reach, skew, False)
    places = jnp.arange(amount)

    def named(sizes, turn):
        used = int((sizes > 0).sum())
        fixed = max(1, used // 4)
        moved = fixed + (places - fixed + turn * (used - fixed)) % max(1, amount - fixed)
        return jnp.zeros((amount,), jnp.int32).at[order[jnp.where(places < fixed, places, moved)]].set(jnp.asarray(sizes, jnp.int32))

    sizes = jnp.where(number % 4 == 0, named(packed, number // 4), named(common, number - number // 4 - 1))
    mixed = jax.random.permutation(jax.random.fold_in(own, 3), amount)
    donor, sink = mixed[0:amount // 2 * 2:2], mixed[1:amount // 2 * 2:2]
    margin = jnp.minimum(sizes[donor] - 1, reach - sizes[sink]) // 2
    margin = jnp.where((donor == order[0]) | (sink == order[0]) | (sizes[sink] == 0), 0, jnp.maximum(margin, 0))
    moved = jax.random.randint(jax.random.fold_in(own, 4), (amount // 2,), 0, 1 << 20) % (margin + 1)
    sizes = sizes.at[donor].add(-moved).at[sink].add(moved)
    items = jnp.searchsorted(jnp.cumsum(sizes), jnp.arange(rows * top), side="right").astype(jnp.int32)
    table = items.reshape(top, rows).T
    table = table[jax.random.permutation(jax.random.fold_in(own, 1), rows)]
    turn = jax.random.randint(jax.random.fold_in(own, 2), (rows, 1), 0, top)
    return jnp.take_along_axis(table, (jnp.arange(top)[None, :] + turn) % top, axis=1)


def load_shares(amount, total, most, slope, full):
    portions = [(1 << 20) // math.isqrt(rank ** slope) + 1 for rank in range(1, amount + 1)]
    largest = most if full else min(most, max(-(-total // amount), total * portions[0] // sum(portions)))
    least = 1 if total - largest >= amount - 1 else 0
    holding, surplus = [largest] + [least] * (amount - 1), total - largest - least * (amount - 1)
    while surplus > 0:
        free = [i for i in range(1, amount) if holding[i] < largest] or [i for i in range(1, amount) if holding[i] < most]
        pool, remaining = sum([portions[i] for i in free]), surplus
        for i in free:
            more = min(most - holding[i], max(1, remaining * portions[i] // pool), surplus)
            holding[i] = holding[i] + more
            surplus = surplus - more
    return np.array(holding)


def gaussian(rng, dims, spread, most, shards=(), kind=jnp.bfloat16):
    factor_of = level_of(rng, dims, shards, -0.22, 0.18) if shards else 1.0
    array = jax.random.normal(rng, dims, jnp.float32) * spread * factor_of
    return jnp.minimum(jnp.maximum(array, -most), most).astype(kind)


def setup_inputs(seed: int = 0, part: int = 0) -> dict:
    streams_of = jax.random.split(jax.random.key(seed), 8)
    part_splits = jax.random.split(jax.random.fold_in(streams_of[7], part), 8)
    tokens = gaussian(part_splits[0], (TOKENS, D), 1.0, 6.0, ((0, 16),))
    expert_ids_keys = jax.random.split(jax.random.fold_in(part_splits[1], 1), TOKENS // TOK_DEV)
    expert_ids_turns = jax.random.permutation(jax.random.fold_in(part_splits[1], 3), TOKENS // TOK_DEV)
    expert_ids = jax.vmap(lambda own, number: assign_block(jax.random.fold_in(part_splits[1], 2), own, number, TOK_DEV, EXPERTS, TOPK, CAP, 2))(expert_ids_keys, expert_ids_turns).reshape((TOKENS, TOPK))
    route_weights = jnp.clip(jnp.exp(math.log(1.0) - 2.9996462 * jax.random.uniform(part_splits[2], (TOKENS, TOPK), jnp.float32) ** level_of(part_splits[2], (TOKENS, TOPK), ((0, 16),), -0.2, 0.2)), 0.049804688, 1.0).astype(jnp.bfloat16)
    smooth = jnp.clip(jnp.exp(jax.random.uniform(streams_of[3], (D,), jnp.float32, math.log(0.3), math.log(3.0))), 0.3, 3.0)
    gate_weight = gaussian(streams_of[4], (EXPERTS, D, FF), D ** -0.5, 0.09375, ((0, 16),))
    up_weight = gaussian(streams_of[5], (EXPERTS, D, FF), D ** -0.5, 0.09375, ((0, 16),))
    down_weight = gaussian(streams_of[6], (EXPERTS, FF, D), FF ** -0.5, 0.21875, ((0, 16),))
    return dict(tokens=tokens, expert_ids=expert_ids, route_weights=route_weights, smooth=smooth, gate_weight=gate_weight, up_weight=up_weight, down_weight=down_weight)


def expert_rows(rows, smooth, gate_one, up_one, down_one):
    folded_gate = (smooth[:, None] * gate_one.astype(jnp.float32)).astype(jnp.bfloat16)
    folded_up = (smooth[:, None] * up_one.astype(jnp.float32)).astype(jnp.bfloat16)
    gate = jnp.dot(rows, folded_gate, preferred_element_type=jnp.float32)
    upper = jnp.dot(rows, folded_up, preferred_element_type=jnp.float32)
    hidden = (jax.nn.silu(gate) * upper).astype(jnp.bfloat16)
    return jnp.dot(hidden, down_one, preferred_element_type=jnp.float32).astype(jnp.bfloat16)


def reference(tokens, expert_ids, route_weights, smooth, gate_weight, up_weight, down_weight):
    limit = N_EP * CAP

    def one_expert(total, inputs):
        number, gate_one, up_one, down_one = inputs
        chosen = expert_ids == number
        picked = jnp.any(chosen, axis=1)
        index = jnp.nonzero(picked, size=limit, fill_value=TOKENS)[0].astype(jnp.int32)
        rows = jnp.take(tokens, index, axis=0, mode="fill", fill_value=0)
        result = expert_rows(rows, smooth, gate_one, up_one, down_one)
        weight = jnp.sum(jnp.where(chosen, route_weights.astype(jnp.float32), jnp.float32(0.0)), axis=1)
        row_weight = jnp.take(weight, index, axis=0, mode="fill", fill_value=0.0)
        total = total.at[index].add(row_weight[:, None] * result.astype(jnp.float32), mode="drop")
        return total, None

    start = jnp.zeros((TOKENS, D), jnp.float32)
    numbers = jnp.arange(EXPERTS, dtype=jnp.int32)
    total, unused = lax.scan(one_expert, start, (numbers, gate_weight, up_weight, down_weight))
    return total.astype(jnp.bfloat16)
```

```python
import jax
import jax.numpy as jnp
from jax import lax
from jax.sharding import PartitionSpec as P

CHUNKS = 2


def shards(tokens, expert_ids, route_weights, smooth, gate_weight, up_weight, down_weight):
    tok_dev, topk = expert_ids.shape
    width = tokens.shape[1]
    experts = lax.axis_size("ep")
    me = lax.axis_index("ep")
    rows = tok_dev // CHUNKS
    chosen = expert_ids[:, :, None] == jnp.arange(experts, dtype=jnp.int32)[None, None, :]
    spread = jnp.sum(
        jnp.where(chosen, route_weights[:, :, None].astype(jnp.float32), 0.0), axis=1
    ).astype(jnp.bfloat16)
    spread_all = lax.all_gather(spread, "ep", axis=0, tiled=False)
    mine = lax.dynamic_slice_in_dim(spread_all, me, 1, axis=2).astype(jnp.float32)
    gathered = [
        lax.all_gather(tokens[i * rows : (i + 1) * rows], "ep", axis=0, tiled=True)
        for i in range(CHUNKS)
    ]
    folded_gate = (smooth[:, None] * gate_weight[0].astype(jnp.float32)).astype(jnp.bfloat16)
    folded_up = (smooth[:, None] * up_weight[0].astype(jnp.float32)).astype(jnp.bfloat16)
    down_one = down_weight[0]
    outs = []
    for i in range(CHUNKS):
        gate = jnp.dot(gathered[i], folded_gate, preferred_element_type=jnp.float32)
        upper = jnp.dot(gathered[i], folded_up, preferred_element_type=jnp.float32)
        hidden = (jax.nn.silu(gate) * upper).astype(jnp.bfloat16)
        result = jnp.dot(hidden, down_one, preferred_element_type=jnp.float32)
        scale = mine[:, i * rows : (i + 1) * rows].reshape(experts * rows, 1)
        part = (result * scale).astype(jnp.bfloat16)
        outs.append(lax.psum_scatter(part, "ep", scatter_dimension=0, tiled=True))
    return jnp.concatenate(outs, axis=0)


def solution(mesh):
    placed = (
        P(("group", "ep"), None),
        P(("group", "ep"), None),
        P(("group", "ep"), None),
        P(),
        P("ep", None, None),
        P("ep", None, None),
        P("ep", None, None),
    )
    return jax.shard_map(
        shards, mesh=mesh, in_specs=placed, out_specs=P(("group", "ep"), None), check_vma=False
    )
```

```python
import jax
import jax.numpy as jnp
from jax import lax
from jax.sharding import PartitionSpec as P

PAD = 128


def shards(tokens, expert_ids, route_weights, smooth, gate_weight, up_weight, down_weight):
    tok_dev, topk = expert_ids.shape
    width = tokens.shape[1]
    experts = lax.axis_size("ep")
    me = lax.axis_index("ep")
    chips = experts // 2
    far = chips // 2
    half = tok_dev // 2
    walk = list(range(0, chips, 2)) + list(range(1, chips, 2))[::-1]
    forward = [
        (walk[i] * 2 + c, walk[(i + 1) % chips] * 2 + c) for i in range(chips) for c in range(2)
    ]
    backward = [(b, a) for a, b in forward]
    swap = [(i, i ^ 1) for i in range(experts)]

    def fwd(x):
        return lax.ppermute(x, "ep", forward)

    def bwd(x):
        return lax.ppermute(x, "ep", backward)

    def other(x):
        return lax.ppermute(x, "ep", swap)

    chosen = expert_ids[:, :, None] == jnp.arange(PAD, dtype=jnp.int32)[None, None, :]
    spread = jnp.sum(
        jnp.where(chosen, route_weights[:, :, None].astype(jnp.float32), 0.0), axis=1
    ).astype(jnp.bfloat16)
    own = jnp.concatenate([tokens, spread], axis=1)

    tall = ((0, PAD), (0, 0))
    folded_gate = jnp.pad(
        (smooth[:, None] * gate_weight[0].astype(jnp.float32)).astype(jnp.bfloat16), tall
    )
    folded_up = jnp.pad(
        (smooth[:, None] * up_weight[0].astype(jnp.float32)).astype(jnp.bfloat16), tall
    )
    down_one = down_weight[0]

    def expert(rows):
        scale = lax.dynamic_slice_in_dim(rows[:, width:], me, 1, axis=1).astype(jnp.float32)
        gate = jnp.dot(rows, folded_gate, preferred_element_type=jnp.float32)
        upper = jnp.dot(rows, folded_up, preferred_element_type=jnp.float32)
        hidden = (jax.nn.silu(gate) * upper).astype(jnp.bfloat16)
        result = jnp.dot(hidden, down_one, preferred_element_type=jnp.float32)
        return (result * scale).astype(jnp.bfloat16)

    def add(*xs):
        total = xs[0].astype(jnp.float32)
        for x in xs[1:]:
            total = total + x.astype(jnp.float32)
        return total.astype(jnp.bfloat16)

    def process(*blocks):
        mine = jnp.concatenate(blocks, axis=0)
        part = expert(jnp.concatenate([mine, other(mine)], axis=0))
        return add(part[: mine.shape[0]], other(part[mine.shape[0] :]))

    behind, ahead = [own], [own]
    for _ in range(far - 1):
        behind.append(fwd(behind[-1]))
        ahead.append(bwd(ahead[-1]))
    behind.append(fwd(behind[-1][:half]))
    ahead.append(bwd(ahead[-1][half:]))

    here = process(own)
    to_behind, to_ahead = {}, {}
    for d in range(1, far):
        both = process(behind[d], ahead[d])
        to_behind[d], to_ahead[d] = both[:tok_dev], both[tok_dev:]
    last = process(behind[far], ahead[far])

    up_sum = fwd(last[:half])
    down_sum = bwd(last[half:])
    for d in range(far - 1, 0, -1):
        if d == far - 1:
            a, b = to_ahead[d], to_behind[d]
            up_sum = jnp.concatenate([add(a[:half], up_sum), a[half:]], axis=0)
            down_sum = jnp.concatenate([b[:half], add(b[half:], down_sum)], axis=0)
        else:
            up_sum = add(to_ahead[d], up_sum)
            down_sum = add(to_behind[d], down_sum)
        up_sum, down_sum = fwd(up_sum), bwd(down_sum)
    return add(here, up_sum, down_sum)


def solution(mesh):
    placed = (
        P(("group", "ep"), None),
        P(("group", "ep"), None),
        P(("group", "ep"), None),
        P(),
        P("ep", None, None),
        P("ep", None, None),
        P("ep", None, None),
    )
    return jax.shard_map(
        shards, mesh=mesh, in_specs=placed, out_specs=P(("group", "ep"), None), check_vma=False
    )
```

```python
import jax
import jax.numpy as jnp
from jax import lax
from jax.experimental import pallas as pl
from jax.experimental.pallas import tpu as pltpu
from jax.sharding import PartitionSpec as P

PAD = 128


def ffn_body(a_ref, b_ref, sa_ref, sb_ref, gate_ref, up_ref, down_ref, oa_ref, ob_ref, acc_ref):
    step = pl.program_id(0)
    steps = pl.num_programs(0)
    width = oa_ref.shape[1]
    tile = 512
    for n, (x_ref, s_ref, o_ref) in enumerate(
        ((a_ref, sa_ref, oa_ref), (b_ref, sb_ref, ob_ref))
    ):
        gate = jnp.dot(x_ref[...], gate_ref[...], preferred_element_type=jnp.float32)
        upper = jnp.dot(x_ref[...], up_ref[...], preferred_element_type=jnp.float32)
        hidden = (gate / (1.0 + jnp.exp(-gate)) * upper).astype(jnp.bfloat16)

        for j in range(width // tile):
            cols = pl.ds(j * tile, tile)
            part = jnp.dot(hidden, down_ref[:, cols], preferred_element_type=jnp.float32)

            @pl.when(step == 0)
            def _():
                acc_ref[n, :, cols] = part

            @pl.when((step > 0) & (step < steps - 1))
            def _():
                acc_ref[n, :, cols] += part

            @pl.when(step == steps - 1)
            def _():
                o_ref[:, cols] = ((acc_ref[n, :, cols] + part) * s_ref[...]).astype(o_ref.dtype)


def ffn(a, b, scale_a, scale_b, folded_gate, folded_up, down_one):
    rows = a.shape[0]
    width, hidden = folded_gate.shape
    block = 256
    steps = hidden // block
    whole = lambda i: (0, 0)
    out = jax.ShapeDtypeStruct((rows, width), jnp.bfloat16)
    return pl.pallas_call(
        ffn_body,
        grid=(steps,),
        in_specs=[
            pl.BlockSpec((rows, width), whole),
            pl.BlockSpec((rows, width), whole),
            pl.BlockSpec((rows, 1), whole),
            pl.BlockSpec((rows, 1), whole),
            pl.BlockSpec((width, block), lambda i: (0, i)),
            pl.BlockSpec((width, block), lambda i: (0, i)),
            pl.BlockSpec((block, width), lambda i: (i, 0)),
        ],
        out_specs=[pl.BlockSpec((rows, width), whole)] * 2,
        out_shape=[out, out],
        scratch_shapes=[pltpu.VMEM((2, rows, width), jnp.float32)],
        cost_estimate=pl.CostEstimate(
            flops=12 * rows * width * hidden,
            bytes_accessed=6 * width * hidden + 8 * rows * width,
            transcendentals=2 * rows * hidden,
        ),
        compiler_params=pltpu.CompilerParams(vmem_limit_bytes=48 * 1024 * 1024),
    )(a, b, scale_a, scale_b, folded_gate, folded_up, down_one)


def shards(tokens, expert_ids, route_weights, smooth, gate_weight, up_weight, down_weight):
    tok_dev, topk = expert_ids.shape
    width = tokens.shape[1]
    experts = lax.axis_size("ep")
    me = lax.axis_index("ep")
    chips = experts // 2
    far = chips // 2
    half = tok_dev // 2
    walk = list(range(0, chips, 2)) + list(range(1, chips, 2))[::-1]
    forward = [
        (walk[i] * 2 + c, walk[(i + 1) % chips] * 2 + c) for i in range(chips) for c in range(2)
    ]
    backward = [(b, a) for a, b in forward]
    swap = [(i, i ^ 1) for i in range(experts)]

    def fwd(x):
        return lax.ppermute(x, "ep", forward)

    def bwd(x):
        return lax.ppermute(x, "ep", backward)

    def other(x):
        return lax.ppermute(x, "ep", swap)

    chosen = expert_ids[:, :, None] == jnp.arange(PAD, dtype=jnp.int32)[None, None, :]
    spread = jnp.sum(
        jnp.where(chosen, route_weights[:, :, None].astype(jnp.float32), 0.0), axis=1
    ).astype(jnp.bfloat16)
    own = jnp.concatenate([tokens, spread], axis=1)

    folded_gate = (smooth[:, None] * gate_weight[0].astype(jnp.float32)).astype(jnp.bfloat16)
    folded_up = (smooth[:, None] * up_weight[0].astype(jnp.float32)).astype(jnp.bfloat16)
    down_one = down_weight[0]

    def scale_of(rows):
        mine = jnp.arange(PAD, dtype=jnp.int32)[None, :] == me
        tail = rows[:, width:].astype(jnp.float32)
        return jnp.sum(jnp.where(mine, tail, 0.0), axis=1, keepdims=True)

    def add(*xs):
        total = xs[0].astype(jnp.float32)
        for x in xs[1:]:
            total = total + x.astype(jnp.float32)
        return total.astype(jnp.bfloat16)

    def compute(*blocks):
        mine = jnp.concatenate(blocks, axis=0) if len(blocks) > 1 else blocks[0]
        theirs = other(mine)
        return ffn(
            mine, theirs, scale_of(mine), scale_of(theirs), folded_gate, folded_up, down_one
        )

    behind, ahead = [own], [own]
    parts = [compute(own)]
    for d in range(1, far + 1):
        x, y = behind[-1], ahead[-1]
        if d >= 2:
            x, y, parts[d - 2] = lax.optimization_barrier((x, y, parts[d - 2]))
        if d == far:
            x, y = x[:half], y[half:]
        behind.append(fwd(x))
        ahead.append(bwd(y))
        parts.append(compute(behind[d], ahead[d]))

    sums = [add(p[0], other(p[1])) for p in parts]
    here, last = sums[0], sums[far]
    to_behind = {d: sums[d][:tok_dev] for d in range(1, far)}
    to_ahead = {d: sums[d][tok_dev:] for d in range(1, far)}

    up_sum = fwd(last[:half])
    down_sum = bwd(last[half:])
    for d in range(far - 1, 0, -1):
        if d == far - 1:
            a, b = to_ahead[d], to_behind[d]
            up_sum = jnp.concatenate([add(a[:half], up_sum), a[half:]], axis=0)
            down_sum = jnp.concatenate([b[:half], add(b[half:], down_sum)], axis=0)
        else:
            up_sum = add(to_ahead[d], up_sum)
            down_sum = add(to_behind[d], down_sum)
        up_sum, down_sum = fwd(up_sum), bwd(down_sum)
    return add(here, up_sum, down_sum)


def solution(mesh):
    placed = (
        P(("group", "ep"), None),
        P(("group", "ep"), None),
        P(("group", "ep"), None),
        P(),
        P("ep", None, None),
        P("ep", None, None),
        P("ep", None, None),
    )
    return jax.shard_map(
        shards, mesh=mesh, in_specs=placed, out_specs=P(("group", "ep"), None), check_vma=False
    )
```

```python
import jax
import jax.numpy as jnp
from jax import lax
from jax.experimental import pallas as pl
from jax.experimental.pallas import tpu as pltpu
from jax.sharding import PartitionSpec as P

PAD = 128


def ffn_body(a_ref, b_ref, sa_ref, sb_ref, gate_ref, up_ref, down_ref, oa_ref, ob_ref, acc_ref):
    step = pl.program_id(0)
    steps = pl.num_programs(0)
    width = oa_ref.shape[1]
    tile = 512
    for n, (x_ref, s_ref, o_ref) in enumerate(
        ((a_ref, sa_ref, oa_ref), (b_ref, sb_ref, ob_ref))
    ):
        gate = jnp.dot(x_ref[...], gate_ref[...], preferred_element_type=jnp.float32)
        upper = jnp.dot(x_ref[...], up_ref[...], preferred_element_type=jnp.float32)
        hidden = (gate / (1.0 + jnp.exp(-gate)) * upper).astype(jnp.bfloat16)

        for j in range(width // tile):
            cols = pl.ds(j * tile, tile)
            part = jnp.dot(hidden, down_ref[:, cols], preferred_element_type=jnp.float32)

            @pl.when(step == 0)
            def _():
                acc_ref[n, :, cols] = part

            @pl.when((step > 0) & (step < steps - 1))
            def _():
                acc_ref[n, :, cols] += part

            @pl.when(step == steps - 1)
            def _():
                o_ref[:, cols] = ((acc_ref[n, :, cols] + part) * s_ref[...]).astype(o_ref.dtype)


def ffn(a, b, scale_a, scale_b, folded_gate, folded_up, down_one):
    rows = a.shape[0]
    width, hidden = folded_gate.shape
    block = 256
    steps = hidden // block
    whole = lambda i: (0, 0)
    out = jax.ShapeDtypeStruct((rows, width), jnp.bfloat16)
    return pl.pallas_call(
        ffn_body,
        grid=(steps,),
        in_specs=[
            pl.BlockSpec((rows, width), whole),
            pl.BlockSpec((rows, width), whole),
            pl.BlockSpec((rows, 1), whole),
            pl.BlockSpec((rows, 1), whole),
            pl.BlockSpec((width, block), lambda i: (0, i)),
            pl.BlockSpec((width, block), lambda i: (0, i)),
            pl.BlockSpec((block, width), lambda i: (i, 0)),
        ],
        out_specs=[pl.BlockSpec((rows, width), whole)] * 2,
        out_shape=[out, out],
        scratch_shapes=[pltpu.VMEM((2, rows, width), jnp.float32)],
        cost_estimate=pl.CostEstimate(
            flops=12 * rows * width * hidden,
            bytes_accessed=6 * width * hidden + 8 * rows * width,
            transcendentals=2 * rows * hidden,
        ),
        compiler_params=pltpu.CompilerParams(vmem_limit_bytes=48 * 1024 * 1024),
    )(a, b, scale_a, scale_b, folded_gate, folded_up, down_one)


def shards(tokens, expert_ids, route_weights, smooth, gate_weight, up_weight, down_weight):
    tok_dev, topk = expert_ids.shape
    width = tokens.shape[1]
    experts = lax.axis_size("ep")
    me = lax.axis_index("ep")
    chips = experts // 2
    far = chips // 2
    half = tok_dev // 2
    walk = list(range(0, chips, 2)) + list(range(1, chips, 2))[::-1]
    forward = [
        (walk[i] * 2 + c, walk[(i + 1) % chips] * 2 + c) for i in range(chips) for c in range(2)
    ]
    backward = [(b, a) for a, b in forward]
    swap = [(i, i ^ 1) for i in range(experts)]

    def fwd(x):
        return lax.ppermute(x, "ep", forward)

    def bwd(x):
        return lax.ppermute(x, "ep", backward)

    def other(x):
        return lax.ppermute(x, "ep", swap)

    chosen = expert_ids[:, :, None] == jnp.arange(PAD, dtype=jnp.int32)[None, None, :]
    spread = jnp.sum(
        jnp.where(chosen, route_weights[:, :, None].astype(jnp.float32), 0.0), axis=1
    ).astype(jnp.bfloat16)
    own = jnp.concatenate([tokens, spread], axis=1)

    folded_gate = (smooth[:, None] * gate_weight[0].astype(jnp.float32)).astype(jnp.bfloat16)
    folded_up = (smooth[:, None] * up_weight[0].astype(jnp.float32)).astype(jnp.bfloat16)
    down_one = down_weight[0]

    def scale_of(rows):
        mine = jnp.arange(PAD, dtype=jnp.int32)[None, :] == me
        tail = rows[:, width:].astype(jnp.float32)
        return jnp.sum(jnp.where(mine, tail, 0.0), axis=1, keepdims=True)

    def add(*xs):
        total = xs[0].astype(jnp.float32)
        for x in xs[1:]:
            total = total + x.astype(jnp.float32)
        return total.astype(jnp.bfloat16)

    def pair(*blocks):
        mine = jnp.concatenate(blocks, axis=0) if len(blocks) > 1 else blocks[0]
        return mine, other(mine)

    def compute(mine, theirs):
        kept, sent = ffn(
            mine, theirs, scale_of(mine), scale_of(theirs), folded_gate, folded_up, down_one
        )
        return add(kept, other(sent))

    x, y = own, own
    pairs = [pair(own)]
    near = None
    for d in range(1, far + 1):
        if d == far:
            x, y = x[:half], y[half:]
        x, y = fwd(x), bwd(y)
        pairs.append(pair(x, y))
        if d == 1:
            near = compute(*pairs[1])
    last = compute(*pairs[far])

    up_sum, down_sum = last[:half], last[half:]
    here = None
    for d in range(far - 1, 0, -1):
        mine, theirs = pairs[d] if d > 1 else pairs[0]
        mine, theirs, up_sum, down_sum = lax.optimization_barrier(
            (mine, theirs, up_sum, down_sum)
        )
        both = compute(mine, theirs)
        if d == 1:
            here, both = both, near
        b, a = both[:tok_dev], both[tok_dev:]
        up_sum, down_sum = fwd(up_sum), bwd(down_sum)
        if d == far - 1:
            up_sum = jnp.concatenate([add(a[:half], up_sum), a[half:]], axis=0)
            down_sum = jnp.concatenate([b[:half], add(b[half:], down_sum)], axis=0)
        else:
            up_sum, down_sum = add(a, up_sum), add(b, down_sum)
    return add(here, fwd(up_sum), bwd(down_sum))


def solution(mesh):
    placed = (
        P(("group", "ep"), None),
        P(("group", "ep"), None),
        P(("group", "ep"), None),
        P(),
        P("ep", None, None),
        P("ep", None, None),
        P("ep", None, None),
    )
    return jax.shard_map(
        shards, mesh=mesh, in_specs=placed, out_specs=P(("group", "ep"), None), check_vma=False
    )
```
